32 devices in a mesh: section: 4 (over y, x), shard: 8 (over z, core).
Axes of the slice: x: 2, y: 2, z: 4, core: 2. Of those that a mesh axis runs over, the one named last changes fastest.
Arguments:
- section_inputs: bfloat16 [4, 2, 384, 16384], P('section', None, None, 'shard'), may hold values from -12 to 12
- top_grad: bfloat16 [2, 384, 16384], P(None, None, 'shard'), may hold values from -6 to 6
- norm_gain: float32 [4, 16384], P('section', 'shard'), may hold values from 0.1 to 1.9
- key_grad: bfloat16 [4, 2, 384, 512], P('section'), may hold values from -18 to 18
- value_grad: bfloat16 [4, 2, 384, 512], P('section'), may hold values from -6 to 6
- key_weight: bfloat16 [4, 512, 16384], P('section', None, 'shard'), may hold values from -0.046875 to 0.046875
- value_weight: bfloat16 [4, 512, 16384], P('section', None, 'shard'), may hold values from -0.046875 to 0.046875
- first_codes: int32 [4, 2, 512, 16384], P('section', None, None, 'shard'), may hold values from 0 to 15
- second_codes: int32 [4, 2, 512, 16384], P('section', None, None, 'shard'), may hold values from 0 to 15
- first_scale: float32 [4, 2, 512, 128], P('section', None, None, 'shard'), may hold values from 2.4414063e-05 to 0.00024414062
- second_scale: float32 [4, 2, 512, 128], P('section', None, None, 'shard'), may hold values from 1.4901161e-09 to 1.4901161e-08
Outputs:
- direction: float32 [4, 2, 512, 16384], P('section', None, None, 'shard')
- first_ratio: float32 [4, 2, 512, 16384], P('section', None, None, 'shard')
- second_ratio: float32 [4, 2, 512, 16384], P('section', None, None, 'shard')
- leaving: bfloat16 [4, 2, 384, 16384], P('section', None, None, 'shard')
The draws below stay inside these ranges and needn't reach their ends.
Inputs may be any that keep to these rules, and one draw needn't show every extreme that they name: `first_codes`: codes follow the encoding of the steps.
All inputs are finite; a program needn't handle non-finite values. Where the reference program divides by a largest or mean magnitude, that divisor is 1e-20 or more.
Results may differ from the reference program's by a relative error of at most 0.0085.
The reference program's roundings to bfloat16 on the way (of `normed`) count: a program that leaves them out, or rounds other values in their place, can miss the bound.
Values may be sent and summed in bfloat16 or wider, within the bound.
A program may use at most 128 MiB of HBM per device.

```python
import math
import jax
import jax.numpy as jnp
from jax import lax

D = 16384
TOK = 384
MB = 2
QB = 128
STEP = 20
KVW = 512
N_SECTION = 4


def joint_draw(key):
    keys = jax.random.split(jax.random.fold_in(key, 41), 5)
    shape = (N_SECTION, MB, TOK, D)
    ramp = 1.0 + 2.0 * jnp.arange(N_SECTION, dtype=jnp.float32) / max(N_SECTION - 1, 1)
    keys_grad = jnp.clip(jax.random.normal(keys[0], (N_SECTION, MB, TOK, KVW)) * ramp[:, None, None, None], -18.0, 18.0)
    weight = jnp.clip(jax.random.normal(keys[1], (N_SECTION, KVW, D)), -6.0, 6.0) * D ** (-0.5)

    def project_section(pair):
        return jnp.dot(pair[0].reshape(MB * TOK, KVW), pair[1], precision=lax.Precision.HIGHEST)
    along = lax.map(project_section, (keys_grad, weight)).reshape(shape)
    along = along / ramp[:, None, None, None] * (D / KVW) ** 0.5
    feature = jnp.arange(D, dtype=jnp.float32) / (D - 1)
    column_scale = jnp.exp(jax.random.uniform(keys[2], (D,), minval=math.log(0.3), maxval=0.0)) * (1.0 + 2.0 * feature)
    row_scale = jnp.exp(jax.random.uniform(keys[3], (N_SECTION, MB, TOK, 1), minval=math.log(0.5), maxval=math.log(2.0)))
    noise = jax.random.normal(keys[4], shape)
    inputs = jnp.clip(noise * column_scale * row_scale + 1.5 * along, -12.0, 12.0)
    return (inputs, keys_grad, weight)


def draw_section_inputs(key, part):
    return joint_draw(key)[0].astype(jnp.float32).astype(jnp.bfloat16)


def draw_key_grad(key, part):
    return joint_draw(key)[1].astype(jnp.float32).astype(jnp.bfloat16)


def draw_key_weight(key, part):
    return joint_draw(key)[2].astype(jnp.float32).astype(jnp.bfloat16)


def with_ends(array, stream_key, least, high):
    shape = array.shape
    index_at = [jax.random.randint(jax.random.fold_in(stream_key, axis), (), 0, shape[axis]) for axis in range(len(shape))]
    array = array.at[tuple(index_at)].set(least)
    longest = shape.index(max(shape))
    index_at[longest] = (index_at[longest] + 1) % shape[longest]
    return array.at[tuple(index_at)].set(high)


def block_levels(stream_key, dims, shards, low, largest):
    def one(dim, shards_of):
        steps = jax.random.uniform(jax.random.fold_in(jax.random.fold_in(stream_key, 6), dim), (shards_of,), jnp.float32, low / len(shards), largest / len(shards))
        return jnp.repeat(jnp.exp(steps), dims[dim] // shards_of).reshape((-1,) + (1,) * (len(dims) - dim - 1))

    level = one(*shards[0])
    for cut in shards[1:]:
        level = level * one(*cut)
    return level


def centred(own_key, shape, deviation, reach, shards=(), held_as=jnp.bfloat16):
    drawn = jax.random.normal(own_key, shape, jnp.float32) * deviation
    if len(shards) > 0:
        drawn = block_levels(own_key, shape, shards, -0.22, 0.18) * drawn
    return jnp.clip(drawn, min=-reach, max=reach).astype(held_as)


def setup_inputs(seed: int = 0) -> dict:
    splits = jax.random.split(jax.random.key(seed), 12)
    return {
        "section_inputs": draw_section_inputs(jax.random.fold_in(splits[11], 71), 0),
        "top_grad": centred(splits[1], (MB, TOK, D), 1.0, 6.0, ((2, 8),)),
        "norm_gain": jnp.clip(1.0 + 0.18 * jax.random.normal(splits[2], (N_SECTION, D), jnp.float32), 0.1, 1.9),
        "key_grad": draw_key_grad(jax.random.fold_in(splits[11], 71), 0),
        "value_grad": centred(splits[4], (N_SECTION, MB, TOK, KVW), 1.0, 6.0, ((0, 4),)),
        "key_weight": draw_key_weight(jax.random.fold_in(splits[11], 71), 0),
        "value_weight": centred(splits[6], (N_SECTION, KVW, D), D ** -0.5, 0.046875, ((0, 4), (2, 8))),
        "first_codes": with_ends(jax.random.randint(splits[7], (N_SECTION, 2, KVW, D), 0, 16), jax.random.fold_in(splits[7], 1), 0, 15).astype(jnp.int32),
        "second_codes": with_ends(jax.random.randint(splits[8], (N_SECTION, 2, KVW, D), 0, 16), jax.random.fold_in(splits[8], 1), 0, 15).astype(jnp.int32),
        "first_scale": jnp.clip(jnp.exp(math.log(0.00024414062) - 2.3025851 * jax.random.uniform(splits[9], (N_SECTION, 2, KVW, D // QB), jnp.float32) ** block_levels(splits[9], (N_SECTION, 2, KVW, D // QB), ((0, 4), (3, 8)), -0.2, 0.2)), 2.441406286379788e-05, 0.00024414062),
        "second_scale": jnp.clip(jnp.exp(math.log(1.4901161193847656e-08) - 2.3025851 * jax.random.uniform(splits[10], (N_SECTION, 2, KVW, D // QB), jnp.float32) ** block_levels(splits[10], (N_SECTION, 2, KVW, D // QB), ((0, 4), (3, 8)), -0.2, 0.2)), 1.4901161415892261e-09, 1.4901161193847656e-08),
    }


beta_one = 0.9
beta_two = 0.95
clip_norm = 1.0

def optimizer(gradients, square_total, first_codes, second_codes, first_scale, second_scale):
    clip_factor = jnp.minimum(1.0, clip_norm / (jnp.sqrt(square_total) + 1e-06))
    clipped = clip_factor * gradients
    sign_part = 1.0 - 2.0 * (first_codes // 8).astype(jnp.float32)
    first_old = jnp.repeat(first_scale, QB, axis=-1) * sign_part * jnp.exp2(-(first_codes % 8).astype(jnp.float32))
    second_old = jnp.repeat(second_scale, QB, axis=-1) * jnp.exp2(-second_codes.astype(jnp.float32))
    first_new = beta_one * first_old + (1.0 - beta_one) * clipped
    second_new = beta_two * second_old + (1.0 - beta_two) * clipped * clipped
    bias_one = 1.0 - beta_one ** STEP
    bias_two = 1.0 - beta_two ** STEP
    direction = first_new / bias_one / (jnp.sqrt(second_new / bias_two) + 1e-08)
    blocks = clipped.reshape(clipped.shape[:-1] + (clipped.shape[-1] // QB, QB))
    first_bound = beta_one * first_scale + (1.0 - beta_one) * lax.optimization_barrier(jnp.max(jnp.abs(blocks), axis=-1))
    second_bound = beta_two * second_scale + (1.0 - beta_two) * lax.optimization_barrier(jnp.max(blocks * blocks, axis=-1))
    first_ratio = first_new / jnp.repeat(first_bound, QB, axis=-1)
    second_ratio = second_new / jnp.repeat(second_bound, QB, axis=-1)
    return (direction, first_ratio, second_ratio)

def reference(section_inputs, top_grad, norm_gain, key_grad, value_grad, key_weight, value_weight, first_codes, second_codes, first_scale, second_scale):
    row_count = MB * TOK
    running = top_grad.reshape(row_count, D).astype(jnp.float32)
    leaving_list = [None] * N_SECTION
    grad_list = [None] * N_SECTION
    for section_num in range(N_SECTION - 1, -1, -1):
        inputs = section_inputs[section_num].reshape(row_count, D)
        inputs_f = inputs.astype(jnp.float32)
        keys_rows = key_grad[section_num].reshape(row_count, KVW)
        values_rows = value_grad[section_num].reshape(row_count, KVW)
        gain = norm_gain[section_num]
        d_normed = jnp.dot(keys_rows, key_weight[section_num], preferred_element_type=jnp.float32) + jnp.dot(values_rows, value_weight[section_num], preferred_element_type=jnp.float32)
        power = lax.optimization_barrier(jnp.sum(inputs_f * inputs_f, axis=1))
        root = 1.0 / jnp.sqrt(power / D + 1e-05)
        normed = (inputs_f * root[:, None] * gain).astype(jnp.bfloat16)
        row_dot = lax.optimization_barrier(jnp.sum(inputs_f * gain * d_normed, axis=1))
        input_grad = gain * d_normed * root[:, None] - inputs_f * (root * root * root * row_dot / D)[:, None]
        running = running + input_grad
        leaving_list[section_num] = running.astype(jnp.bfloat16).reshape(MB, TOK, D)
        grad_list[section_num] = jnp.stack([jnp.dot(keys_rows.T, normed, preferred_element_type=jnp.float32), jnp.dot(values_rows.T, normed, preferred_element_type=jnp.float32)])
    gradients = jnp.stack(grad_list)
    square_total = jnp.sum(gradients * gradients)
    direction, first_ratio, second_ratio = optimizer(gradients, square_total, first_codes, second_codes, first_scale, second_scale)
    return (direction, first_ratio, second_ratio, jnp.stack(leaving_list))
```

```python
import functools

import jax
import jax.numpy as jnp
from jax import lax
from jax.experimental import pallas as pl
from jax.experimental.pallas import tpu as pltpu
from jax.sharding import PartitionSpec as P

D = 16384
QB = 128
STEP = 20

beta_one = 0.9
beta_two = 0.95
clip_norm = 1.0
MIB = 1 << 20


def optimizer_body(
    total_ref, grad_ref, first_ref, second_ref, fscale_ref, sscale_ref, dir_ref, fr_ref, sr_ref
):
    clip_factor = jnp.minimum(1.0, clip_norm / (jnp.sqrt(total_ref[0:1, 0:1]) + 1e-06))
    inv_one = 1.0 / (1.0 - beta_one**STEP)
    inv_two = 1.0 / (1.0 - beta_two**STEP)
    fscale = fscale_ref[0]
    sscale = sscale_ref[0]
    for block in range(grad_ref.shape[2] // QB):
        cols = slice(block * QB, (block + 1) * QB)
        grad = clip_factor * grad_ref[0, :, cols]
        peak = jnp.max(jnp.abs(grad), axis=1, keepdims=True)
        f_scale = fscale[:, block : block + 1]
        s_scale = sscale[:, block : block + 1]
        f_code = first_ref[0, :, cols]
        s_code = second_ref[0, :, cols]
        f_power = lax.shift_right_logical(jnp.full_like(f_code, 128), f_code & 7)
        f_power = jnp.where(f_code >= 8, -f_power, f_power).astype(jnp.float32)
        s_power = lax.shift_right_logical(jnp.full_like(s_code, 32768), s_code).astype(jnp.float32)
        first_new = (f_scale * (beta_one / 128.0)) * f_power + (1.0 - beta_one) * grad
        second_new = (s_scale * (beta_two / 32768.0)) * s_power + (1.0 - beta_two) * grad * grad
        f_bound = 1.0 / (beta_one * f_scale + (1.0 - beta_one) * peak)
        s_bound = 1.0 / (beta_two * s_scale + (1.0 - beta_two) * peak * peak)
        dir_ref[0, :, cols] = first_new * inv_one / (jnp.sqrt(second_new * inv_two) + 1e-08)
        fr_ref[0, :, cols] = first_new * f_bound
        sr_ref[0, :, cols] = second_new * s_bound


def optimizer(total, gradients, first_codes, second_codes, first_scale, second_scale):
    stacks, features, width = gradients.shape
    rows = features // 4
    while rows > 128 and rows % 2 == 0:
        rows //= 2
    scales = width // QB

    def spec(columns):
        return pl.BlockSpec((1, rows, columns), lambda i, j: (i, j, 0))

    out = jax.ShapeDtypeStruct(gradients.shape, jnp.float32)
    count = stacks * features * width
    return pl.pallas_call(
        optimizer_body,
        grid=(stacks, features // rows),
        in_specs=[pl.BlockSpec((8, 128), lambda i, j: (0, 0))]
        + [spec(width)] * 3
        + [spec(scales)] * 2,
        out_specs=[spec(width)] * 3,
        out_shape=[out] * 3,
        compiler_params=pltpu.CompilerParams(vmem_limit_bytes=40 * MIB),
        cost_estimate=pl.CostEstimate(
            flops=40 * count, bytes_accessed=24 * count, transcendentals=2 * count
        ),
    )(total, gradients, first_codes, second_codes, first_scale, second_scale)


def project(left, right):
    return lax.dot_general(
        left, right, (((0,), (0,)), ((), ())), preferred_element_type=jnp.float32
    )


def on_device(
    section_inputs,
    top_grad,
    norm_gain,
    key_grad,
    value_grad,
    key_weight,
    value_weight,
    first_codes,
    second_codes,
    first_scale,
    second_scale,
):
    micro_count, token_count, width_local = top_grad.shape
    row_count = micro_count * token_count
    section_count = lax.axis_size("section")
    inputs = section_inputs[0].reshape(row_count, width_local)
    inputs_f = inputs.astype(jnp.float32)
    gain = norm_gain[0]
    keys_rows = key_grad[0].reshape(row_count, key_grad.shape[3])
    values_rows = value_grad[0].reshape(row_count, value_grad.shape[3])
    d_normed = jnp.dot(keys_rows, key_weight[0], preferred_element_type=jnp.float32) + jnp.dot(
        values_rows, value_weight[0], preferred_element_type=jnp.float32
    )
    local_power = jnp.sum(inputs_f * inputs_f, axis=1)
    local_dot = jnp.sum(inputs_f * gain * d_normed, axis=1)
    power, row_dot = lax.psum((local_power, local_dot), "shard")
    root = 1.0 / jnp.sqrt(power / D + 1e-05)
    normed = (inputs_f * root[:, None] * gain).astype(jnp.bfloat16)
    input_grad = (
        gain * d_normed * root[:, None] - inputs_f * (root * root * root * row_dot / D)[:, None]
    ).astype(jnp.bfloat16)
    block_rows = row_count // section_count
    gradients = jnp.stack([project(keys_rows, normed), project(values_rows, normed)])
    square_total = lax.psum(jnp.sum(gradients * gradients), ("section", "shard"))
    split_rows = input_grad.reshape(section_count, block_rows, width_local)
    by_section = lax.all_to_all(split_rows, "section", split_axis=0, concat_axis=0, tiled=True)
    top_rows = top_grad.reshape(section_count, block_rows, width_local)
    running = lax.dynamic_index_in_dim(
        top_rows, lax.axis_index("section"), 0, keepdims=False
    ).astype(jnp.float32)
    suffix = [None] * section_count
    for section in range(section_count - 1, -1, -1):
        running = running + by_section[section].astype(jnp.float32)
        suffix[section] = running.astype(jnp.bfloat16)
    returned = lax.all_to_all(
        jnp.stack(suffix), "section", split_axis=0, concat_axis=0, tiled=True
    )
    leaving = returned.reshape(1, micro_count, token_count, width_local)
    direction, first_ratio, second_ratio = optimizer(
        jnp.broadcast_to(square_total, (8, 128)),
        gradients,
        first_codes[0],
        second_codes[0],
        first_scale[0],
        second_scale[0],
    )
    return (direction[None], first_ratio[None], second_ratio[None], leaving)


def solution(mesh):
    sharded = P("section", None, None, "shard")
    whole_rows = P("section", None, None, None)
    return jax.shard_map(
        on_device,
        mesh=mesh,
        in_specs=(
            sharded,
            P(None, None, "shard"),
            P("section", "shard"),
            whole_rows,
            whole_rows,
            P("section", None, "shard"),
            P("section", None, "shard"),
            sharded,
            sharded,
            sharded,
            sharded,
        ),
        out_specs=(sharded, sharded, sharded, sharded),
        check_vma=False,
    )
```

```python
import functools

import jax
import jax.numpy as jnp
from jax import lax
from jax.experimental import pallas as pl
from jax.experimental.pallas import tpu as pltpu
from jax.sharding import PartitionSpec as P

D = 16384
QB = 128
STEP = 20

beta_one = 0.9
beta_two = 0.95
clip_norm = 1.0
MIB = 1 << 20


def optimizer_body(
    total_ref, grad_ref, first_ref, second_ref, fscale_ref, sscale_ref, dir_ref, fr_ref, sr_ref
):
    clip_factor = jnp.minimum(1.0, clip_norm / (jnp.sqrt(total_ref[0:1, 0:1]) + 1e-06))
    inv_one = 1.0 / (1.0 - beta_one**STEP)
    inv_two = 1.0 / (1.0 - beta_two**STEP)
    fscale = fscale_ref[0]
    sscale = sscale_ref[0]
    for block in range(grad_ref.shape[2] // QB):
        cols = slice(block * QB, (block + 1) * QB)
        grad = clip_factor * grad_ref[0, :, cols]
        peak = jnp.max(jnp.abs(grad), axis=1, keepdims=True)
        f_scale = fscale[:, block : block + 1]
        s_scale = sscale[:, block : block + 1]
        f_code = first_ref[0, :, cols]
        s_code = second_ref[0, :, cols]
        f_power = lax.shift_right_logical(jnp.full_like(f_code, 128), f_code & 7)
        f_power = jnp.where(f_code >= 8, -f_power, f_power).astype(jnp.float32)
        s_power = lax.shift_right_logical(jnp.full_like(s_code, 32768), s_code).astype(jnp.float32)
        first_new = (f_scale * (beta_one / 128.0)) * f_power + (1.0 - beta_one) * grad
        second_new = (s_scale * (beta_two / 32768.0)) * s_power + (1.0 - beta_two) * grad * grad
        f_bound = 1.0 / (beta_one * f_scale + (1.0 - beta_one) * peak)
        s_bound = 1.0 / (beta_two * s_scale + (1.0 - beta_two) * peak * peak)
        dir_ref[0, :, cols] = first_new * inv_one / (jnp.sqrt(second_new * inv_two) + 1e-08)
        fr_ref[0, :, cols] = first_new * f_bound
        sr_ref[0, :, cols] = second_new * s_bound


def optimizer(total, gradients, first_codes, second_codes, first_scale, second_scale):
    stacks, features, width = gradients.shape
    rows = features // 4
    while rows > 128 and rows % 2 == 0:
        rows //= 2
    scales = width // QB

    def spec(columns):
        return pl.BlockSpec((1, rows, columns), lambda i, j: (i, j, 0))

    out = jax.ShapeDtypeStruct(gradients.shape, jnp.float32)
    count = stacks * features * width
    return pl.pallas_call(
        optimizer_body,
        grid=(stacks, features // rows),
        in_specs=[pl.BlockSpec((8, 128), lambda i, j: (0, 0))]
        + [spec(width)] * 3
        + [spec(scales)] * 2,
        out_specs=[spec(width)] * 3,
        out_shape=[out] * 3,
        compiler_params=pltpu.CompilerParams(vmem_limit_bytes=40 * MIB),
        cost_estimate=pl.CostEstimate(
            flops=40 * count, bytes_accessed=24 * count, transcendentals=2 * count
        ),
    )(total, gradients, first_codes, second_codes, first_scale, second_scale)


def reduce_body(axes, x_ref, out_ref, *scratch):
    barrier = pltpu.get_barrier_semaphore()
    peers = 0
    for axis, size in axes:
        me = lax.axis_index(axis)
        for step in range(1, size):
            pl.semaphore_signal(
                barrier,
                inc=1,
                device_id={axis: lax.rem(me + step, size)},
                device_id_type=pl.DeviceIdType.MESH,
            )
            peers += 1
    pl.semaphore_wait(barrier, peers)
    value = x_ref[...]
    for at, (axis, size) in enumerate(axes):
        slots, send, receive = scratch[3 * at : 3 * at + 3]
        me = lax.axis_index(axis)
        slots[0] = value
        copies = []
        for step in range(1, size):
            copy = pltpu.make_async_remote_copy(
                src_ref=slots.at[0],
                dst_ref=slots.at[step],
                send_sem=send.at[step],
                recv_sem=receive.at[step],
                device_id={axis: lax.rem(me + step, size)},
                device_id_type=pl.DeviceIdType.MESH,
            )
            copy.start()
            copies.append(copy)
        for copy in copies:
            copy.wait()
        value = slots[0]
        for step in range(1, size):
            value = value + slots[step]
    out_ref[...] = value


def reduce_over(x, axis_names, identity):
    axes = [(axis, lax.axis_size(axis)) for axis in axis_names]
    if max(size for _, size in axes) > 8:
        return lax.psum(x, axis_names)
    scratch = []
    for _, size in axes:
        scratch += [
            pltpu.VMEM((size,) + x.shape, jnp.float32),
            pltpu.SemaphoreType.DMA((size,)),
            pltpu.SemaphoreType.DMA((size,)),
        ]
    vmem = pl.BlockSpec(memory_space=pltpu.VMEM)
    return pl.pallas_call(
        functools.partial(reduce_body, axes),
        in_specs=[vmem],
        out_specs=vmem,
        out_shape=jax.ShapeDtypeStruct(x.shape, jnp.float32),
        scratch_shapes=scratch,
        compiler_params=pltpu.CompilerParams(collective_id=identity, has_side_effects=True),
        cost_estimate=pl.CostEstimate(flops=10000, bytes_accessed=1 << 20, transcendentals=0),
    )(x)


def project(left, right):
    return lax.dot_general(
        left, right, (((0,), (0,)), ((), ())), preferred_element_type=jnp.float32
    )


def on_device(
    section_inputs,
    top_grad,
    norm_gain,
    key_grad,
    value_grad,
    key_weight,
    value_weight,
    first_codes,
    second_codes,
    first_scale,
    second_scale,
):
    micro_count, token_count, width_local = top_grad.shape
    row_count = micro_count * token_count
    section_count = lax.axis_size("section")
    inputs = section_inputs[0].reshape(row_count, width_local)
    inputs_f = inputs.astype(jnp.float32)
    gain = norm_gain[0]
    keys_rows = key_grad[0].reshape(row_count, key_grad.shape[3])
    values_rows = value_grad[0].reshape(row_count, value_grad.shape[3])
    d_normed = jnp.dot(keys_rows, key_weight[0], preferred_element_type=jnp.float32) + jnp.dot(
        values_rows, value_weight[0], preferred_element_type=jnp.float32
    )
    local_power = jnp.sum(inputs_f * inputs_f, axis=1)
    local_dot = jnp.sum(inputs_f * gain * d_normed, axis=1)
    lanes = jnp.stack([local_power, local_dot]).reshape(-1, 128)
    lane_rows = lanes.shape[0]
    lanes = jnp.pad(lanes, ((0, -lane_rows % 8), (0, 0)))
    power, row_dot = reduce_over(lanes, ("shard",), 0)[:lane_rows].reshape(2, row_count)
    root = 1.0 / jnp.sqrt(power / D + 1e-05)
    normed = (inputs_f * root[:, None] * gain).astype(jnp.bfloat16)
    input_grad = (
        gain * d_normed * root[:, None] - inputs_f * (root * root * root * row_dot / D)[:, None]
    ).astype(jnp.bfloat16)
    block_rows = row_count // section_count
    gradients = jnp.stack([project(keys_rows, normed), project(values_rows, normed)])
    split_rows = input_grad.reshape(section_count, block_rows, width_local)
    by_section = lax.all_to_all(split_rows, "section", split_axis=0, concat_axis=0, tiled=True)
    partial = jnp.broadcast_to(jnp.sum(gradients * gradients), (8, 128))
    square_total = reduce_over(partial, ("shard", "section"), 1)
    by_section, square_total = lax.optimization_barrier((by_section, square_total))
    top_rows = top_grad.reshape(section_count, block_rows, width_local)
    running = lax.dynamic_index_in_dim(
        top_rows, lax.axis_index("section"), 0, keepdims=False
    ).astype(jnp.float32)
    suffix = [None] * section_count
    for section in range(section_count - 1, -1, -1):
        running = running + by_section[section].astype(jnp.float32)
        suffix[section] = running.astype(jnp.bfloat16)
    suffix, square_total = lax.optimization_barrier((jnp.stack(suffix), square_total))
    returned = lax.all_to_all(
        suffix, "section", split_axis=0, concat_axis=0, tiled=True
    )
    leaving = returned.reshape(1, micro_count, token_count, width_local)
    direction, first_ratio, second_ratio = optimizer(
        square_total,
        gradients,
        first_codes[0],
        second_codes[0],
        first_scale[0],
        second_scale[0],
    )
    return (direction[None], first_ratio[None], second_ratio[None], leaving)


def solution(mesh):
    sharded = P("section", None, None, "shard")
    whole_rows = P("section", None, None, None)
    return jax.shard_map(
        on_device,
        mesh=mesh,
        in_specs=(
            sharded,
            P(None, None, "shard"),
            P("section", "shard"),
            whole_rows,
            whole_rows,
            P("section", None, "shard"),
            P("section", None, "shard"),
            sharded,
            sharded,
            sharded,
            sharded,
        ),
        out_specs=(sharded, sharded, sharded, sharded),
        check_vma=False,
    )
```
